32 devices in a mesh: section: 2 (over x), shard: 4 (over y, core), replica: 4 (over z).
Axes of the slice: x: 2, y: 2, z: 4, core: 2. Of those that a mesh axis runs over, the one named last changes fastest.
Arguments:
- inputs: bfloat16 [4096, 576], P(('shard', 'replica')), may hold values from -6 to 6
- segments: int32 [32, 128], P(('shard', 'replica')), may hold values from 0 to 3, never falling along the last dimension, each value on 1 to 64 neighbouring positions
- cotangent: bfloat16 [4096, 576], P(('shard', 'replica')), may hold values from -6 to 6
- attn_gain: float32 [2, 576], P('section'), may hold values from 0.1 to 1.9
- qkv_weight: bfloat16 [2, 576, 960], P('section', 'shard'), may hold values from -0.25 to 0.25
- out_weight: bfloat16 [2, 576, 576], P('section', 'shard'), may hold values from -0.75 to 0.75
- ffn_gain: float32 [2, 576], P('section'), may hold values from 0.1 to 1.9
- gate_up_weight: bfloat16 [2, 576, 3072], P('section', 'shard'), may hold values from -0.25 to 0.25
- down_weight: bfloat16 [2, 1536, 576], P('section', 'shard'), may hold values from -0.15625 to 0.15625
Outputs:
- activations: bfloat16 [2, 4096, 576], P('section', ('shard', 'replica'))
- input_grads: bfloat16 [2, 4096, 576], P('section', ('shard', 'replica'))
- attn_gain_grad: float32 [2, 576], P('section', 'shard')
- qkv_grad: float32 [2, 576, 960], P('section', 'shard')
- out_grad: float32 [2, 576, 576], P('section', 'shard')
- ffn_gain_grad: float32 [2, 576], P('section', 'shard')
- gate_up_grad: float32 [2, 576, 3072], P('section', 'shard')
- down_grad: float32 [2, 1536, 576], P('section', 'shard')
The draws below stay inside these ranges and needn't reach their ends.
Inputs may be any that keep to these rules, and one draw needn't show every extreme that they name: `segments`: in each sequence the document numbers never fall; every document has 1 to 64 tokens, and some document exactly 64.
All inputs are finite; a program needn't handle non-finite values.
Results may differ from the reference program's by a relative error of at most 0.02.
Values may be sent and summed in bfloat16 or wider, within the bound.
A program may use at most 128 MiB of HBM per device.

```python
import math
import jax
import jax.numpy as jnp
import numpy as np
from jax import lax

D = 576
HEADS = 9
KV = 3
HD = 64
FF = 1536
SEQ = 128
MB = 2
QKV = 960
SEQS = 32
TOKENS = 4096
N_SECTION = 2
N_SHARD = 4


def level_of(own_key, dims, shards, smallest, top_value):
    level = 1.0
    for position, shards_of in shards:
        steps = jax.random.uniform(jax.random.fold_in(jax.random.fold_in(own_key, 6), position), (shards_of,), jnp.float32, smallest / len(shards), top_value / len(shards))
        level = level * jnp.repeat(jnp.exp(steps), dims[position] // shards_of).reshape((-1,) + (1,) * (len(dims) - 1 - position))
    return level


def length_profile(amount, total, reach, skew):
    loads = [(1 << 20) // math.isqrt(grade ** skew) + 1 for grade in range(2, amount + 1)]
    spare, holding = total - reach - (amount - 1), [1] * (amount - 1)
    while spare > 0:
        candidates = [i for i in range(amount - 1) if holding[i] < reach]
        mass, budget = sum([loads[i] for i in candidates]), spare
        for i in candidates:
            extra = min(reach - holding[i], max(1, budget * loads[i] // mass), spare)
            holding[i] = holding[i] + extra
            spare = spare - extra
    return np.array([reach] + holding)


def uneven(rng, count, total, most, skew):
    if count == 2:
        one = jax.random.randint(rng, (), max(1, total - most), min(most, total - 1) + 1)
        return jnp.stack([one, total - one])
    lengths = jnp.asarray(length_profile(count, total, most, skew), jnp.int32)
    pairs = (count - 1) // 2
    giver, sink = lengths[1:1 + 2 * pairs:2], lengths[2:2 + 2 * pairs:2]
    margin = jnp.minimum(giver - 1, most - sink)
    moved = jax.random.randint(jax.random.fold_in(rng, 1), (pairs,), 0, 1 << 20) % (margin + 1)
    lengths = lengths.at[1:1 + 2 * pairs:2].set(giver - moved).at[2:2 + 2 * pairs:2].set(sink + moved)
    return lengths[jax.random.permutation(jax.random.fold_in(rng, 2), count)]


def gaussian(stream_key, extent, deviation, bound, shards=(), kind=jnp.bfloat16):
    drawn = deviation * jax.random.normal(stream_key, extent, jnp.float32)
    if shards:
        drawn = drawn * level_of(stream_key, extent, shards, -0.22, 0.18)
    return jnp.clip(drawn, -bound, bound).astype(kind)


def setup_inputs(seed: int = 0) -> dict:
    key_list = jax.random.split(jax.random.key(seed), 10)
    inputs = gaussian(key_list[0], (TOKENS, D), 1.0, 6.0, ((0, 16),))
    segments = jax.vmap(lambda own: jnp.searchsorted(jnp.cumsum(uneven(own, 4, SEQ, SEQ // 2, 1)), jnp.arange(SEQ), side="right"))(jax.random.split(key_list[1], SEQS)).reshape((SEQS, SEQ)).astype(jnp.int32)
    cotangent = gaussian(key_list[2], (TOKENS, D), 1.0, 6.0, ((0, 16),))
    attn_gain = jnp.clip(1.0 + 0.18 * jax.random.normal(key_list[3], (N_SECTION, D), jnp.float32), 0.1, 1.9)
    qkv_weight = gaussian(key_list[4], (N_SECTION, D, QKV), D ** -0.5, 0.25, ((0, 2), (1, 4)))
    out_weight = gaussian(key_list[5], (N_SECTION, D, D), (D // 8) ** -0.5, 0.75, ((0, 2), (1, 4)))
    ffn_gain = jnp.clip(1.0 + 0.18 * jax.random.normal(key_list[6], (N_SECTION, D), jnp.float32), 0.1, 1.9)
    gate_up_weight = gaussian(key_list[7], (N_SECTION, D, 2 * FF), D ** -0.5, 0.25, ((0, 2), (1, 4)))
    down_weight = gaussian(key_list[8], (N_SECTION, FF, D), FF ** -0.5, 0.15625, ((0, 2), (1, 4)))
    return dict(inputs=inputs, segments=segments, cotangent=cotangent, attn_gain=attn_gain, qkv_weight=qkv_weight, out_weight=out_weight, ffn_gain=ffn_gain, gate_up_weight=gate_up_weight, down_weight=down_weight)


norm_epsilon = 1e-05
rope_base = 100000.0
masked_value = -1e+30

@jax.custom_vjp
def low(v):
    return lax.optimization_barrier(v.astype(jnp.bfloat16)).astype(jnp.float32)

@jax.custom_vjp
def low_back(v):
    return v

def low_keep(v):
    return (low(v), None)

def low_pass(kept, grad):
    return (grad,)

def back_keep(v):
    return (v, None)

def back_low(kept, grad):
    return (low(grad),)
low.defvjp(low_keep, low_pass)
low_back.defvjp(back_keep, back_low)

def geometry(segment_ids):
    count_cols = segment_ids.shape[-1]
    column = jnp.arange(count_cols, dtype=jnp.int32)
    previous = jnp.concatenate([segment_ids[..., :1], segment_ids[..., :-1]], axis=-1)
    doc_marks = jnp.where(segment_ids != previous, column, 0).astype(jnp.int32)
    doc_starts = lax.cummax(doc_marks, axis=doc_marks.ndim - 1)
    positions = (column - doc_starts).astype(jnp.float32)
    allowed = (segment_ids[..., :, None] == segment_ids[..., None, :]) & (column[:, None] >= column[None, :])
    half_width = HD // 2
    frequency = jnp.exp(-(jnp.arange(half_width, dtype=jnp.float32) * (2.0 / HD)) * math.log(rope_base))
    angles = positions[..., None] * frequency
    return (allowed, jnp.cos(angles), jnp.sin(angles))

def rotate(tensor, cosine_table, sine_table):
    half_width = tensor.shape[-1] // 2
    first_half = tensor[..., :half_width]
    second_half = tensor[..., half_width:]
    cosine_table = cosine_table[..., None, :]
    sine_table = sine_table[..., None, :]
    return jnp.concatenate([first_half * cosine_table - second_half * sine_table, second_half * cosine_table + first_half * sine_table], axis=-1)

def project(activ, matrix):
    return jnp.einsum('gsd,de->gse', activ, matrix, precision=lax.Precision.HIGHEST)

def scaled(stream, gain_row):
    return stream * lax.rsqrt(lax.optimization_barrier(jnp.mean(stream * stream, axis=-1, keepdims=True)) + norm_epsilon) * gain_row

def layer(stream, gain_attn, qkv_layer, out_layer, gain_ffn, gate_up_layer, down_layer, allowed, cosine_table, sine_table):
    group_count, length = (stream.shape[0], stream.shape[1])
    normed = low(scaled(stream, gain_attn))
    projected = low_back(project(normed, qkv_layer))
    query_rows = projected[..., :HEADS * HD].reshape(group_count, length, HEADS, HD)
    key_rows = projected[..., HEADS * HD:(HEADS + KV) * HD].reshape(group_count, length, KV, HD)
    value_rows = projected[..., (HEADS + KV) * HD:].reshape(group_count, length, KV, HD)
    query_rows = low(rotate(query_rows, cosine_table, sine_table)).reshape(group_count, length, KV, HEADS // KV, HD)
    key_rows = low(rotate(key_rows, cosine_table, sine_table))
    value_rows = low(value_rows)
    score_scale = HD ** (-0.5)
    scores = low_back(jnp.einsum('gqkrd,gtkd->gkrqt', query_rows, key_rows, precision=lax.Precision.HIGHEST) * score_scale)
    scores = jnp.where(allowed[:, None, None], scores, masked_value)
    attn_probs = low(jax.nn.softmax(scores, axis=-1))
    attended = jnp.einsum('gkrqt,gtkd->gqkrd', attn_probs, value_rows, precision=lax.Precision.HIGHEST)
    attended = low_back(low(attended.reshape(group_count, length, HEADS * HD)))
    middle = stream + low_back(project(attended, out_layer))
    ffn_normed = low(scaled(middle, gain_ffn))
    gate_up = low_back(project(ffn_normed, gate_up_layer))
    hidden = low(jax.nn.silu(gate_up[..., :FF]) * gate_up[..., FF:])
    return middle + low_back(project(hidden, down_layer))

def forward(first_input, params, probes, allowed, cosine_table, sine_table):
    attn_gains, qkv_layers, out_layers, ffn_gains, gate_up_layers, down_layers = params
    stream = first_input
    outputs = []
    for layer_index in range(N_SECTION):
        if layer_index > 0:
            stream = low_back(low(stream) + probes[layer_index - 1])
        stream = layer(stream, attn_gains[layer_index], qkv_layers[layer_index], out_layers[layer_index], ffn_gains[layer_index], gate_up_layers[layer_index], down_layers[layer_index], allowed, cosine_table, sine_table)
        outputs.append(low(stream))
    return (stream, jnp.stack(outputs))

def reference(inputs, segments, cotangent, attn_gain, qkv_weight, out_weight, ffn_gain, gate_up_weight, down_weight):
    group_size = MB * N_SHARD
    group_count = SEQS // group_size
    group_inputs = inputs.astype(jnp.float32).reshape(group_count, group_size, SEQ, D)
    group_cots = cotangent.astype(jnp.float32).reshape(group_count, group_size, SEQ, D)
    group_segments = segments.reshape(group_count, group_size, SEQ)
    params = tuple((member.astype(jnp.float32) for member in (attn_gain, qkv_weight, out_weight, ffn_gain, gate_up_weight, down_weight)))

    def one_group(totals, slices):
        first_input, cot_rows, segment_rows = slices
        allowed, cosine_table, sine_table = geometry(segment_rows)
        probes = jnp.zeros((N_SECTION - 1, group_size, SEQ, D), jnp.float32)

        def closure(start_rows, weights_in, probe_rows):
            return forward(start_rows, weights_in, probe_rows, allowed, cosine_table, sine_table)
        final_rows, pullback, layer_outputs = jax.vjp(closure, first_input, params, probes, has_aux=True)
        input_grad, param_grads, probe_grads = pullback(cot_rows)
        totals = jax.tree.map(lambda left, right: left + right, totals, param_grads)
        input_grads = jnp.concatenate([input_grad[None], probe_grads], axis=0)
        return (totals, (layer_outputs, input_grads))
    zero_grads = jax.tree.map(lambda member: jnp.zeros(member.shape, jnp.float32), params)
    totals, (layer_outputs, input_grads) = lax.scan(one_group, zero_grads, (group_inputs, group_cots, group_segments))
    layer_outputs = jnp.transpose(layer_outputs, (1, 0, 2, 3, 4)).reshape(N_SECTION, TOKENS, D)
    input_grads = jnp.transpose(input_grads, (1, 0, 2, 3, 4)).reshape(N_SECTION, TOKENS, D)
    return (layer_outputs.astype(jnp.bfloat16), input_grads.astype(jnp.bfloat16), totals[0], totals[1], totals[2], totals[3], totals[4], totals[5])
```

```python
import functools
import math

import jax
import jax.numpy as jnp
from jax import lax
from jax.experimental import pallas as pl
from jax.experimental.pallas import tpu as pltpu
from jax.sharding import PartitionSpec as P

HEADS = 9
KV = 3
HD = 64
FF = 1536


norm_epsilon = 1e-05
rope_base = 100000.0
masked_value = -1e30


def geometry(segment_ids):
    count_cols = segment_ids.shape[-1]
    column = jnp.arange(count_cols, dtype=jnp.int32)
    previous = jnp.concatenate([segment_ids[..., :1], segment_ids[..., :-1]], axis=-1)
    doc_marks = jnp.where(segment_ids != previous, column, 0)
    doc_starts = lax.cummax(doc_marks, axis=doc_marks.ndim - 1)
    positions = (column - doc_starts).astype(jnp.float32)
    allowed = (segment_ids[..., :, None] == segment_ids[..., None, :]) & (
        column[:, None] >= column[None, :]
    )
    half_width = HD // 2
    frequency = jnp.exp(
        -(jnp.arange(half_width, dtype=jnp.float32) * (2.0 / HD)) * math.log(rope_base)
    )
    angles = positions[..., None] * frequency
    return (allowed, jnp.cos(angles), jnp.sin(angles))


def rotate(tensor, cosine_table, sine_table):
    half_width = tensor.shape[-1] // 2
    first_half = tensor[..., :half_width]
    second_half = tensor[..., half_width:]
    cosine_table = cosine_table[..., None, :]
    sine_table = sine_table[..., None, :]
    return jnp.concatenate(
        [
            first_half * cosine_table - second_half * sine_table,
            second_half * cosine_table + first_half * sine_table,
        ],
        axis=-1,
    )


def unrotate(tensor, cosine_table, sine_table):
    half_width = tensor.shape[-1] // 2
    first_half = tensor[..., :half_width]
    second_half = tensor[..., half_width:]
    cosine_table = cosine_table[..., None, :]
    sine_table = sine_table[..., None, :]
    return jnp.concatenate(
        [
            first_half * cosine_table + second_half * sine_table,
            second_half * cosine_table - first_half * sine_table,
        ],
        axis=-1,
    )


def masked_scores(query_rows, key_rows, allowed):
    scores = jnp.einsum(
        "gqkrd,gtkd->gkrqt", query_rows, key_rows, preferred_element_type=jnp.float32
    ) * HD ** (-0.5)
    return jnp.where(allowed[:, None, None], scores, masked_value)


def norm_back(residual, stream, inverse, gain_row, grad_out):
    grad_gain = jnp.sum(grad_out * stream * inverse, axis=0)
    grad_hat = grad_out * gain_row
    inner = jnp.mean(grad_hat * stream, axis=-1, keepdims=True)
    return (residual + inverse * (grad_hat - stream * inverse * inverse * inner), grad_gain)


def layer_forward(layer_in, weights, geom):
    gain_attn, qkv_layer, out_layer, gain_ffn, gate_up_layer, down_layer = weights
    allowed, cosine_table, sine_table = geom
    groups, length = allowed.shape[:2]
    stream = layer_in.astype(jnp.float32)
    inv_attn = lax.rsqrt(jnp.mean(stream * stream, axis=-1, keepdims=True) + norm_epsilon)
    normed = (stream * inv_attn * gain_attn).astype(jnp.bfloat16)
    projected = jnp.dot(normed, qkv_layer, preferred_element_type=jnp.float32)
    projected = projected.reshape(groups, length, HEADS + 2 * KV, HD)
    query_rows = projected[:, :, :HEADS]
    key_rows = projected[:, :, HEADS : HEADS + KV]
    value_rows = projected[:, :, HEADS + KV :].astype(jnp.bfloat16)
    query_rows = (
        rotate(query_rows, cosine_table, sine_table)
        .astype(jnp.bfloat16)
        .reshape(groups, length, KV, HEADS // KV, HD)
    )
    key_rows = rotate(key_rows, cosine_table, sine_table).astype(jnp.bfloat16)
    scores = masked_scores(query_rows, key_rows, allowed)
    row_max = jnp.max(scores, axis=-1, keepdims=True)
    row_exp = jnp.exp(scores - row_max)
    row_sum = jnp.sum(row_exp, axis=-1, keepdims=True)
    attn_probs = row_exp / row_sum
    attended = jnp.einsum(
        "gkrqt,gtkd->gqkrd",
        attn_probs.astype(jnp.bfloat16),
        value_rows,
        preferred_element_type=jnp.float32,
    )
    attended = attended.reshape(groups * length, HEADS * HD).astype(jnp.bfloat16)
    middle = stream + jnp.dot(attended, out_layer, preferred_element_type=jnp.float32)
    inv_ffn = lax.rsqrt(jnp.mean(middle * middle, axis=-1, keepdims=True) + norm_epsilon)
    ffn_normed = (middle * inv_ffn * gain_ffn).astype(jnp.bfloat16)
    gate_up = jnp.dot(ffn_normed, gate_up_layer, preferred_element_type=jnp.float32)
    hidden = (jax.nn.silu(gate_up[:, :FF]) * gate_up[:, FF:]).astype(jnp.bfloat16)
    result = middle + jnp.dot(hidden, down_layer, preferred_element_type=jnp.float32)
    stored = (
        stream,
        inv_attn,
        normed,
        query_rows,
        key_rows,
        value_rows,
        attn_probs,
        attended,
        middle,
        inv_ffn,
        ffn_normed,
        gate_up,
        hidden,
    )
    return (result, stored)


def layer_backward(incoming, weights, geom, stored):
    gain_attn, qkv_layer, out_layer, gain_ffn, gate_up_layer, down_layer = weights
    allowed, cosine_table, sine_table = geom
    groups, length = allowed.shape[:2]
    (
        stream,
        inv_attn,
        normed,
        query_rows,
        key_rows,
        value_rows,
        attn_probs,
        attended,
        middle,
        inv_ffn,
        ffn_normed,
        gate_up,
        hidden,
    ) = stored
    out_rounded = incoming.astype(jnp.bfloat16)
    grad_hidden = jnp.einsum(
        "sd,fd->sf", out_rounded, down_layer, preferred_element_type=jnp.float32
    )
    gate_part = gate_up[:, :FF]
    up_part = gate_up[:, FF:]
    gate_sigmoid = jax.nn.sigmoid(gate_part)
    gate_silu = gate_part * gate_sigmoid
    grad_gate = grad_hidden * up_part * gate_sigmoid * (1.0 + gate_part * (1.0 - gate_sigmoid))
    grad_gu = jnp.concatenate([grad_gate, grad_hidden * gate_silu], axis=-1).astype(jnp.bfloat16)
    grad_fnorm = jnp.einsum("se,de->sd", grad_gu, gate_up_layer, preferred_element_type=jnp.float32)
    grad_middle, grad_gain_ffn = norm_back(incoming, middle, inv_ffn, gain_ffn, grad_fnorm)
    mid_rounded = grad_middle.astype(jnp.bfloat16)
    grad_att = jnp.einsum("sd,cd->sc", mid_rounded, out_layer, preferred_element_type=jnp.float32)
    grad_att = grad_att.astype(jnp.bfloat16).reshape(groups, length, KV, HEADS // KV, HD)
    grad_values = jnp.einsum(
        "gkrqt,gqkrd->gtkd",
        attn_probs.astype(jnp.bfloat16),
        grad_att,
        preferred_element_type=jnp.float32,
    )
    grad_probs = jnp.einsum(
        "gqkrd,gtkd->gkrqt", grad_att, value_rows, preferred_element_type=jnp.float32
    )
    inner = jnp.sum(attn_probs * grad_probs, axis=-1, keepdims=True)
    grad_scores = (attn_probs * (grad_probs - inner)).astype(jnp.bfloat16)
    grad_query = jnp.einsum(
        "gkrqt,gtkd->gqkrd", grad_scores, key_rows, preferred_element_type=jnp.float32
    ) * HD ** (-0.5)
    grad_keys = jnp.einsum(
        "gkrqt,gqkrd->gtkd", grad_scores, query_rows, preferred_element_type=jnp.float32
    ) * HD ** (-0.5)
    grad_query = unrotate(
        grad_query.reshape(groups, length, HEADS, HD), cosine_table, sine_table
    ).reshape(groups * length, HEADS * HD)
    grad_keys = unrotate(grad_keys, cosine_table, sine_table).reshape(groups * length, KV * HD)
    grad_projected = jnp.concatenate(
        [grad_query, grad_keys, grad_values.reshape(groups * length, KV * HD)], axis=-1
    ).astype(jnp.bfloat16)
    grad_normed = jnp.einsum(
        "se,de->sd", grad_projected, qkv_layer, preferred_element_type=jnp.float32
    )
    grad_stream, grad_gain_attn = norm_back(grad_middle, stream, inv_attn, gain_attn, grad_normed)
    operands = (
        (hidden, out_rounded),
        (ffn_normed, grad_gu),
        (attended, mid_rounded),
        (normed, grad_projected),
    )
    return (grad_stream, (grad_gain_attn, grad_gain_ffn), operands)


GAIN_ROWS = 16
MESH_ID = pl.DeviceIdType.MESH


def split_pieces(shapes):
    pieces = []
    for array, (rows, columns) in enumerate(shapes):
        row_step = 128 if rows > 144 and rows % 128 == 0 else rows
        column_step = 512 if columns > 1024 else columns
        for row in range(0, rows, row_step):
            for column in range(0, columns, column_step):
                pieces.append((array, row, row_step, column, column_step))
    return pieces


def reduce_kernel(pieces, replicas, *refs):
    count = len(pieces) + 1
    lefts, rights, gain_ref = refs[0:4], refs[4:8], refs[8]
    outs, gain_out = refs[9:13], refs[13]
    scratch = refs[14:]
    groups = [scratch[k * count : (k + 1) * count] for k in range(8)]
    send_a, recv_a, keep_a, send_b, recv_b, send_c, recv_c, recv_x = groups
    totals = scratch[8 * count : 9 * count]
    sems = scratch[9 * count :]
    a_out, a_in, b_out, b_in, c_out, c_in, x_out, x_in = sems

    shard = lax.axis_index("shard")
    place = lax.axis_index("replica")
    core = shard % 2
    row_y = shard // 2
    sibling = row_y * 2 + (1 - core)
    across = (1 - row_y) * 2 + core
    half = replicas // 2
    is_left = place < half
    inward = jnp.where(is_left, place + 1, place - 1)
    outward = jnp.where(is_left, place - 1, place + 1)
    is_middle = (place == half - 1) | (place == half)
    has_outer = (place > 0) & (place < replicas - 1)

    barrier = pltpu.get_barrier_semaphore()
    for peer in (sibling, across):
        pl.semaphore_signal(barrier, inc=1, device_id={"shard": peer}, device_id_type=MESH_ID)
    pl.semaphore_signal(barrier, inc=1, device_id={"replica": inward}, device_id_type=MESH_ID)

    @pl.when(has_outer)
    def _():
        pl.semaphore_signal(barrier, inc=1, device_id={"replica": outward}, device_id_type=MESH_ID)

    pl.semaphore_wait(barrier, jnp.where(has_outer, 4, 3))

    def copy(source, target, out_sem, in_sem, device):
        return pltpu.make_async_remote_copy(
            src_ref=source,
            dst_ref=target,
            send_sem=out_sem,
            recv_sem=in_sem,
            device_id=device,
            device_id_type=MESH_ID,
        )

    def copy_a(p):
        return copy(send_a[p], recv_a[p], a_out.at[p], a_in.at[p], {"shard": sibling})

    def copy_b(p):
        return copy(send_b[p], recv_b[p], b_out.at[p], b_in.at[p], {"shard": across})

    def copy_c(p):
        return copy(send_c[p], recv_c[p], c_out.at[p], c_in.at[p], {"replica": inward})

    def copy_middle(p):
        return copy(send_c[p], recv_x[p], c_out.at[p], x_in.at[p], {"replica": inward})

    def copy_x(p):
        return copy(totals[p], recv_x[p], x_out.at[p], x_in.at[p], {"replica": outward})

    def term(p, owner):
        if p == count - 1:
            return gain_ref[owner]
        array, row, rows, column, columns = pieces[p]
        return jnp.dot(
            lefts[array][owner, row : row + rows, :],
            rights[array][:, column : column + columns],
            preferred_element_type=jnp.float32,
        )

    def stage_a(p):
        for y in range(2):
            send_a[p][y] = term(p, 2 * y + (1 - core)).astype(jnp.bfloat16)
        copy_a(p).start()
        for y in range(2):
            keep_a[p][y] = term(p, 2 * y + core)

    def stage_b(p):
        copy_a(p).wait_recv()
        other = 1 - row_y
        send_b[p][...] = (keep_a[p][other] + recv_a[p][other].astype(jnp.float32)).astype(
            jnp.bfloat16
        )
        copy_b(p).start()

    def stage_c(p):
        copy_b(p).wait_recv()
        keep_a[p][0] = (
            keep_a[p][row_y]
            + recv_a[p][row_y].astype(jnp.float32)
            + recv_b[p][...].astype(jnp.float32)
        )

        @pl.when(has_outer)
        def _():
            copy_c(p).wait_recv()
            keep_a[p][0] = keep_a[p][0] + recv_c[p][...].astype(jnp.float32)

        send_c[p][...] = keep_a[p][0].astype(jnp.bfloat16)

        @pl.when(is_middle)
        def _():
            copy_middle(p).start()

        @pl.when(jnp.logical_not(is_middle))
        def _():
            copy_c(p).start()

    def stage_d(p):
        copy_x(p).wait_recv()

        @pl.when(is_middle)
        def _():
            totals[p][...] = (
                send_c[p][...].astype(jnp.float32) + recv_x[p][...].astype(jnp.float32)
            ).astype(jnp.bfloat16)

        @pl.when(jnp.logical_not(is_middle))
        def _():
            totals[p][...] = recv_x[p][...]

        @pl.when(has_outer)
        def _():
            copy_x(p).start()

        total = totals[p][...].astype(jnp.float32)
        if p == count - 1:
            gain_out[...] = total
        else:
            array, row, rows, column, columns = pieces[p]
            outs[array][row : row + rows, column : column + columns] = total

    for step in range(count + 4):
        if step < count:
            stage_a(step)
        if 0 <= step - 1 < count:
            stage_b(step - 1)
        if 0 <= step - 2 < count:
            stage_c(step - 2)
        if 0 <= step - 4 < count:
            stage_d(step - 4)
    for p in range(count):
        copy_a(p).wait_send()
        copy_b(p).wait_send()
        copy_c(p).wait_send()

        @pl.when(has_outer)
        def _(p=p):
            copy_x(p).wait_send()


def reduce_gradients(operands, gains, replicas):
    owners = lax.axis_size("shard")
    lefts, rights, shapes = [], [], []
    for left, right in operands:
        tokens, rows = left.shape
        lefts.append(left.T.reshape(owners, rows // owners, tokens))
        rights.append(right)
        shapes.append((rows // owners, right.shape[1]))
    width = gains[0].shape[0] // owners
    packed = jnp.stack([gain.reshape(owners, width) for gain in gains], axis=1)
    packed = jnp.pad(packed, ((0, 0), (0, GAIN_ROWS - 2), (0, 256 - width)))
    pieces = split_pieces(shapes)
    extents = [(rows, columns) for _, _, rows, _, columns in pieces] + [(GAIN_ROWS, 256)]
    low, full = jnp.bfloat16, jnp.float32
    scratch = []
    for lead, kind in (
        ((2,), low),
        ((2,), low),
        ((2,), full),
        ((), low),
        ((), low),
        ((), low),
        ((), low),
        ((), low),
        ((), low),
    ):
        scratch += [pltpu.VMEM(lead + extent, kind) for extent in extents]
    scratch += [pltpu.SemaphoreType.DMA((len(extents),))] * 8
    vmem = pl.BlockSpec(memory_space=pltpu.VMEM)
    flops = sum(2 * left.shape[0] * left.shape[1] * right.shape[1] for left, right in operands)
    results = pl.pallas_call(
        functools.partial(reduce_kernel, pieces, replicas),
        out_shape=[jax.ShapeDtypeStruct(shape, full) for shape in shapes]
        + [jax.ShapeDtypeStruct((GAIN_ROWS, 256), full)],
        in_specs=[vmem] * 9,
        out_specs=[vmem] * 5,
        scratch_shapes=scratch,
        compiler_params=pltpu.CompilerParams(
            collective_id=1, has_side_effects=True, vmem_limit_bytes=58 * 2**20
        ),
        cost_estimate=pl.CostEstimate(flops=flops, bytes_accessed=2 * 2**20, transcendentals=0),
    )(*lefts, *rights, packed)
    gain_rows = results[4]
    return results[:4], [gain_rows[i : i + 1, :width] for i in range(2)]


def from_behind(block, axis, distance):
    devices = range(lax.axis_size(axis))
    route = [(i - distance, i) for i in devices if i - distance in devices]
    return lax.ppermute(block, axis, route)


def shards(
    inputs,
    segments,
    cotangent,
    attn_gain,
    qkv_weight,
    out_weight,
    ffn_gain,
    gate_up_weight,
    down_weight,
):
    sections = lax.axis_size("section")
    section_index = lax.axis_index("section")
    qkv_full, out_full, gate_up_full, down_full = (
        lax.all_gather(qkv_weight[0], "shard", axis=0, tiled=True),
        lax.all_gather(out_weight[0], "shard", axis=0, tiled=True),
        lax.all_gather(gate_up_weight[0], "shard", axis=0, tiled=True),
        lax.all_gather(down_weight[0], "shard", axis=0, tiled=True),
    )
    weights = (attn_gain[0], qkv_full, out_full, ffn_gain[0], gate_up_full, down_full)
    geom = geometry(segments)
    layer_in = inputs
    for tick in range(sections):
        if tick > 0:
            arrived = from_behind(outgoing, "section", 1)
            layer_in = jnp.where(section_index == 0, inputs, arrived)
        result, stored = layer_forward(layer_in, weights, geom)
        outgoing = result.astype(jnp.bfloat16)
    incoming = cotangent
    for tick in range(sections):
        if tick > 0:
            arrived = from_behind(passed, "section", -1)
            incoming = jnp.where(section_index == sections - 1, cotangent, arrived)
        grad_stream, gain_terms, operands = layer_backward(
            incoming.astype(jnp.float32), weights, geom, stored
        )
        passed = grad_stream.astype(jnp.bfloat16)
    sums, gain_sums = reduce_gradients(operands, gain_terms, lax.axis_size("replica"))
    down_sum, gate_up_sum, out_sum, qkv_sum = sums
    return (
        outgoing[None],
        passed[None],
        gain_sums[0],
        qkv_sum[None],
        out_sum[None],
        gain_sums[1],
        gate_up_sum[None],
        down_sum[None],
    )


def solution(mesh):
    return jax.shard_map(
        shards,
        mesh=mesh,
        in_specs=(
            P(("shard", "replica"), None),
            P(("shard", "replica"), None),
            P(("shard", "replica"), None),
            P("section", None),
            P("section", "shard", None),
            P("section", "shard", None),
            P("section", None),
            P("section", "shard", None),
            P("section", "shard", None),
        ),
        out_specs=(
            P("section", ("shard", "replica"), None),
            P("section", ("shard", "replica"), None),
            P("section", "shard"),
            P("section", "shard", None),
            P("section", "shard", None),
            P("section", "shard"),
            P("section", "shard", None),
            P("section", "shard", None),
        ),
        check_vma=False,
    )
```

```python
import functools
import math

import jax
import jax.numpy as jnp
from jax import lax
from jax.experimental import pallas as pl
from jax.experimental.pallas import tpu as pltpu
from jax.sharding import PartitionSpec as P

HEADS = 9
KV = 3
HD = 64
FF = 1536


norm_epsilon = 1e-05
rope_base = 100000.0
masked_value = -1e30


def geometry(segment_ids):
    count_cols = segment_ids.shape[-1]
    column = jnp.arange(count_cols, dtype=jnp.int32)
    previous = jnp.concatenate([segment_ids[..., :1], segment_ids[..., :-1]], axis=-1)
    doc_marks = jnp.where(segment_ids != previous, column, 0)
    doc_starts = lax.cummax(doc_marks, axis=doc_marks.ndim - 1)
    positions = (column - doc_starts).astype(jnp.float32)
    allowed = (segment_ids[..., :, None] == segment_ids[..., None, :]) & (
        column[:, None] >= column[None, :]
    )
    half_width = HD // 2
    frequency = jnp.exp(
        -(jnp.arange(half_width, dtype=jnp.float32) * (2.0 / HD)) * math.log(rope_base)
    )
    angles = positions[..., None] * frequency
    return (allowed, jnp.cos(angles), jnp.sin(angles))


def rotate(tensor, cosine_table, sine_table):
    half_width = tensor.shape[-1] // 2
    first_half = tensor[..., :half_width]
    second_half = tensor[..., half_width:]
    cosine_table = cosine_table[..., None, :]
    sine_table = sine_table[..., None, :]
    return jnp.concatenate(
        [
            first_half * cosine_table - second_half * sine_table,
            second_half * cosine_table + first_half * sine_table,
        ],
        axis=-1,
    )


def unrotate(tensor, cosine_table, sine_table):
    half_width = tensor.shape[-1] // 2
    first_half = tensor[..., :half_width]
    second_half = tensor[..., half_width:]
    cosine_table = cosine_table[..., None, :]
    sine_table = sine_table[..., None, :]
    return jnp.concatenate(
        [
            first_half * cosine_table + second_half * sine_table,
            second_half * cosine_table - first_half * sine_table,
        ],
        axis=-1,
    )


def masked_scores(query_rows, key_rows, allowed):
    scores = jnp.einsum(
        "gqkrd,gtkd->gkrqt", query_rows, key_rows, preferred_element_type=jnp.float32
    ) * HD ** (-0.5)
    return jnp.where(allowed[:, None, None], scores, masked_value)


def norm_back(residual, stream, inverse, gain_row, grad_out):
    grad_gain = jnp.sum(grad_out * stream * inverse, axis=0)
    grad_hat = grad_out * gain_row
    inner = jnp.mean(grad_hat * stream, axis=-1, keepdims=True)
    return (residual + inverse * (grad_hat - stream * inverse * inverse * inner), grad_gain)


def layer_forward(layer_in, weights, geom):
    gain_attn, qkv_layer, out_layer, gain_ffn, gate_up_layer, down_layer = weights
    allowed, cosine_table, sine_table = geom
    groups, length = allowed.shape[:2]
    stream = layer_in.astype(jnp.float32)
    inv_attn = lax.rsqrt(jnp.mean(stream * stream, axis=-1, keepdims=True) + norm_epsilon)
    normed = (stream * inv_attn * gain_attn).astype(jnp.bfloat16)
    projected = jnp.dot(normed, qkv_layer, preferred_element_type=jnp.float32)
    projected = projected.reshape(groups, length, HEADS + 2 * KV, HD)
    query_rows = projected[:, :, :HEADS]
    key_rows = projected[:, :, HEADS : HEADS + KV]
    value_rows = projected[:, :, HEADS + KV :].astype(jnp.bfloat16)
    query_rows = (
        rotate(query_rows, cosine_table, sine_table)
        .astype(jnp.bfloat16)
        .reshape(groups, length, KV, HEADS // KV, HD)
    )
    key_rows = rotate(key_rows, cosine_table, sine_table).astype(jnp.bfloat16)
    scores = masked_scores(query_rows, key_rows, allowed)
    row_max = jnp.max(scores, axis=-1, keepdims=True)
    row_exp = jnp.exp(scores - row_max)
    row_sum = jnp.sum(row_exp, axis=-1, keepdims=True)
    attn_probs = row_exp / row_sum
    attended = jnp.einsum(
        "gkrqt,gtkd->gqkrd",
        attn_probs.astype(jnp.bfloat16),
        value_rows,
        preferred_element_type=jnp.float32,
    )
    attended = attended.reshape(groups * length, HEADS * HD).astype(jnp.bfloat16)
    middle = stream + jnp.dot(attended, out_layer, preferred_element_type=jnp.float32)
    inv_ffn = lax.rsqrt(jnp.mean(middle * middle, axis=-1, keepdims=True) + norm_epsilon)
    ffn_normed = (middle * inv_ffn * gain_ffn).astype(jnp.bfloat16)
    gate_up = jnp.dot(ffn_normed, gate_up_layer, preferred_element_type=jnp.float32)
    hidden = (jax.nn.silu(gate_up[:, :FF]) * gate_up[:, FF:]).astype(jnp.bfloat16)
    result = middle + jnp.dot(hidden, down_layer, preferred_element_type=jnp.float32)
    stored = (
        stream,
        inv_attn,
        normed,
        query_rows,
        key_rows,
        value_rows,
        attn_probs,
        attended,
        middle,
        inv_ffn,
        ffn_normed,
        gate_up,
        hidden,
    )
    return (result, stored)


def layer_backward(incoming, weights, geom, stored):
    gain_attn, qkv_layer, out_layer, gain_ffn, gate_up_layer, down_layer = weights
    allowed, cosine_table, sine_table = geom
    groups, length = allowed.shape[:2]
    (
        stream,
        inv_attn,
        normed,
        query_rows,
        key_rows,
        value_rows,
        attn_probs,
        attended,
        middle,
        inv_ffn,
        ffn_normed,
        gate_up,
        hidden,
    ) = stored
    out_rounded = incoming.astype(jnp.bfloat16)
    grad_hidden = jnp.einsum(
        "sd,fd->sf", out_rounded, down_layer, preferred_element_type=jnp.float32
    )
    gate_part = gate_up[:, :FF]
    up_part = gate_up[:, FF:]
    gate_sigmoid = jax.nn.sigmoid(gate_part)
    gate_silu = gate_part * gate_sigmoid
    grad_gate = grad_hidden * up_part * gate_sigmoid * (1.0 + gate_part * (1.0 - gate_sigmoid))
    grad_gu = jnp.concatenate([grad_gate, grad_hidden * gate_silu], axis=-1).astype(jnp.bfloat16)
    grad_fnorm = jnp.einsum("se,de->sd", grad_gu, gate_up_layer, preferred_element_type=jnp.float32)
    grad_middle, grad_gain_ffn = norm_back(incoming, middle, inv_ffn, gain_ffn, grad_fnorm)
    mid_rounded = grad_middle.astype(jnp.bfloat16)
    grad_att = jnp.einsum("sd,cd->sc", mid_rounded, out_layer, preferred_element_type=jnp.float32)
    grad_att = grad_att.astype(jnp.bfloat16).reshape(groups, length, KV, HEADS // KV, HD)
    grad_values = jnp.einsum(
        "gkrqt,gqkrd->gtkd",
        attn_probs.astype(jnp.bfloat16),
        grad_att,
        preferred_element_type=jnp.float32,
    )
    grad_probs = jnp.einsum(
        "gqkrd,gtkd->gkrqt", grad_att, value_rows, preferred_element_type=jnp.float32
    )
    inner = jnp.sum(attn_probs * grad_probs, axis=-1, keepdims=True)
    grad_scores = (attn_probs * (grad_probs - inner)).astype(jnp.bfloat16)
    grad_query = jnp.einsum(
        "gkrqt,gtkd->gqkrd", grad_scores, key_rows, preferred_element_type=jnp.float32
    ) * HD ** (-0.5)
    grad_keys = jnp.einsum(
        "gkrqt,gqkrd->gtkd", grad_scores, query_rows, preferred_element_type=jnp.float32
    ) * HD ** (-0.5)
    grad_query = unrotate(
        grad_query.reshape(groups, length, HEADS, HD), cosine_table, sine_table
    ).reshape(groups * length, HEADS * HD)
    grad_keys = unrotate(grad_keys, cosine_table, sine_table).reshape(groups * length, KV * HD)
    grad_projected = jnp.concatenate(
        [grad_query, grad_keys, grad_values.reshape(groups * length, KV * HD)], axis=-1
    ).astype(jnp.bfloat16)
    grad_normed = jnp.einsum(
        "se,de->sd", grad_projected, qkv_layer, preferred_element_type=jnp.float32
    )
    grad_stream, grad_gain_attn = norm_back(grad_middle, stream, inv_attn, gain_attn, grad_normed)
    operands = (
        (hidden, out_rounded),
        (ffn_normed, grad_gu),
        (attended, mid_rounded),
        (normed, grad_projected),
    )
    return (grad_stream, (grad_gain_attn, grad_gain_ffn), operands)


GAIN_ROWS = 16
MESH_ID = pl.DeviceIdType.MESH


def split_pieces(shapes):
    pieces = []
    for array, (rows, columns) in enumerate(shapes):
        row_step = 128 if rows > 144 and rows % 128 == 0 else rows
        column_step = 512 if columns > 1024 else columns
        for row in range(0, rows, row_step):
            for column in range(0, columns, column_step):
                pieces.append((array, row, row_step, column, column_step))
    return pieces


def reduce_kernel(pieces, replicas, *refs):
    count = len(pieces) + 1
    lefts, rights, gain_ref = refs[0:4], refs[4:8], refs[8]
    outs, gain_out = refs[9:13], refs[13]
    scratch = refs[14:]
    groups = [scratch[k * count : (k + 1) * count] for k in range(8)]
    send_a, recv_a, keep_a, send_b, recv_b, send_c, recv_c, recv_x = groups
    totals = scratch[8 * count : 9 * count]
    sems = scratch[9 * count :]
    a_out, a_in, b_out, b_in, c_out, c_in, x_out, x_in = sems

    shard = lax.axis_index("shard")
    place = lax.axis_index("replica")
    core = shard % 2
    row_y = shard // 2
    sibling = row_y * 2 + (1 - core)
    across = (1 - row_y) * 2 + core
    half = replicas // 2
    is_left = place < half
    inward = jnp.where(is_left, place + 1, place - 1)
    outward = jnp.where(is_left, place - 1, place + 1)
    is_middle = (place == half - 1) | (place == half)
    has_outer = (place > 0) & (place < replicas - 1)

    barrier = pltpu.get_barrier_semaphore()
    for peer in (sibling, across):
        pl.semaphore_signal(barrier, inc=1, device_id={"shard": peer}, device_id_type=MESH_ID)
    pl.semaphore_signal(barrier, inc=1, device_id={"replica": inward}, device_id_type=MESH_ID)

    @pl.when(has_outer)
    def _():
        pl.semaphore_signal(barrier, inc=1, device_id={"replica": outward}, device_id_type=MESH_ID)

    pl.semaphore_wait(barrier, jnp.where(has_outer, 4, 3))

    def copy(source, target, out_sem, in_sem, device):
        return pltpu.make_async_remote_copy(
            src_ref=source,
            dst_ref=target,
            send_sem=out_sem,
            recv_sem=in_sem,
            device_id=device,
            device_id_type=MESH_ID,
        )

    def copy_a(p):
        return copy(send_a[p], recv_a[p], a_out.at[p], a_in.at[p], {"shard": sibling})

    def copy_b(p):
        return copy(send_b[p], recv_b[p], b_out.at[p], b_in.at[p], {"shard": across})

    def copy_c(p):
        return copy(send_c[p], recv_c[p], c_out.at[p], c_in.at[p], {"replica": inward})

    def copy_middle(p):
        return copy(send_c[p], recv_x[p], c_out.at[p], x_in.at[p], {"replica": inward})

    def copy_x(p):
        return copy(totals[p], recv_x[p], x_out.at[p], x_in.at[p], {"replica": outward})

    def term(p, owner):
        if p == count - 1:
            return gain_ref[owner]
        array, row, rows, column, columns = pieces[p]
        return jnp.dot(
            lefts[array][owner, row : row + rows, :],
            rights[array][:, column : column + columns],
            preferred_element_type=jnp.float32,
        )

    def stage_a(p):
        for y in range(2):
            send_a[p][y] = term(p, 2 * y + (1 - core)).astype(jnp.bfloat16)
        copy_a(p).start()
        for y in range(2):
            keep_a[p][y] = term(p, 2 * y + core)

    def stage_b(p):
        copy_a(p).wait_recv()
        other = 1 - row_y
        send_b[p][...] = (keep_a[p][other] + recv_a[p][other].astype(jnp.float32)).astype(
            jnp.bfloat16
        )
        copy_b(p).start()

    def stage_c(p):
        copy_b(p).wait_recv()
        keep_a[p][0] = (
            keep_a[p][row_y]
            + recv_a[p][row_y].astype(jnp.float32)
            + recv_b[p][...].astype(jnp.float32)
        )

        @pl.when(has_outer)
        def _():
            copy_c(p).wait_recv()
            keep_a[p][0] = keep_a[p][0] + recv_c[p][...].astype(jnp.float32)

        send_c[p][...] = keep_a[p][0].astype(jnp.bfloat16)

        @pl.when(is_middle)
        def _():
            copy_middle(p).start()

        @pl.when(jnp.logical_not(is_middle))
        def _():
            copy_c(p).start()

    def finish(p):
        @pl.when(has_outer)
        def _():
            copy_x(p).start()

        total = totals[p][...].astype(jnp.float32)
        if p == count - 1:
            gain_out[...] = total
        else:
            array, row, rows, column, columns = pieces[p]
            outs[array][row : row + rows, column : column + columns] = total

    def stage_middle(p):
        copy_x(p).wait_recv()
        totals[p][...] = (
            send_c[p][...].astype(jnp.float32) + recv_x[p][...].astype(jnp.float32)
        ).astype(jnp.bfloat16)
        finish(p)

    def stage_outer(p):
        copy_x(p).wait_recv()
        totals[p][...] = recv_x[p][...]
        finish(p)

    lag_b, lag_c, lag_d, lag_outer = 2, 5, 8, 12
    for step in range(count + lag_outer):
        if step < count:
            stage_a(step)
        if 0 <= step - lag_b < count:
            stage_b(step - lag_b)
        if 0 <= step - lag_c < count:
            stage_c(step - lag_c)
        if 0 <= step - lag_d < count:
            pl.when(is_middle)(functools.partial(stage_middle, step - lag_d))
        if 0 <= step - lag_outer < count:
            pl.when(jnp.logical_not(is_middle))(functools.partial(stage_outer, step - lag_outer))
    for p in range(count):
        copy_a(p).wait_send()
        copy_b(p).wait_send()
        copy_c(p).wait_send()

        @pl.when(has_outer)
        def _(p=p):
            copy_x(p).wait_send()


def reduce_gradients(operands, gains, replicas):
    owners = lax.axis_size("shard")
    lefts, rights, shapes = [], [], []
    for left, right in operands:
        tokens, rows = left.shape
        lefts.append(left.T.reshape(owners, rows // owners, tokens))
        rights.append(right)
        shapes.append((rows // owners, right.shape[1]))
    width = gains[0].shape[0] // owners
    packed = jnp.stack([gain.reshape(owners, width) for gain in gains], axis=1)
    packed = jnp.pad(packed, ((0, 0), (0, GAIN_ROWS - 2), (0, 256 - width)))
    pieces = split_pieces(shapes)
    extents = [(rows, columns) for _, _, rows, _, columns in pieces] + [(GAIN_ROWS, 256)]
    low, full = jnp.bfloat16, jnp.float32
    scratch = []
    for lead, kind in (
        ((2,), low),
        ((2,), low),
        ((2,), full),
        ((), low),
        ((), low),
        ((), low),
        ((), low),
        ((), low),
        ((), low),
    ):
        scratch += [pltpu.VMEM(lead + extent, kind) for extent in extents]
    scratch += [pltpu.SemaphoreType.DMA((len(extents),))] * 8
    vmem = pl.BlockSpec(memory_space=pltpu.VMEM)
    flops = sum(2 * left.shape[0] * left.shape[1] * right.shape[1] for left, right in operands)
    results = pl.pallas_call(
        functools.partial(reduce_kernel, pieces, replicas),
        out_shape=[jax.ShapeDtypeStruct(shape, full) for shape in shapes]
        + [jax.ShapeDtypeStruct((GAIN_ROWS, 256), full)],
        in_specs=[vmem] * 9,
        out_specs=[vmem] * 5,
        scratch_shapes=scratch,
        compiler_params=pltpu.CompilerParams(
            collective_id=1, has_side_effects=True, vmem_limit_bytes=58 * 2**20
        ),
        cost_estimate=pl.CostEstimate(flops=flops, bytes_accessed=2 * 2**20, transcendentals=0),
    )(*lefts, *rights, packed)
    gain_rows = results[4]
    return results[:4], [gain_rows[i : i + 1, :width] for i in range(2)]


def gather_kernel(halves, *refs):
    owned, full = refs[0:4], refs[4:8]
    near_out, near_in, far_out, far_in, side_out, pass_out, pass_in, local = refs[8:]
    shard = lax.axis_index("shard")
    place = lax.axis_index("replica")
    core = shard % 2
    row_y = shard // 2
    sibling = row_y * 2 + (1 - core)
    across = (1 - row_y) * 2 + core
    parity = place % 2
    partner = place + 1 - 2 * parity

    barrier = pltpu.get_barrier_semaphore()
    for peer in ({"shard": sibling}, {"shard": across}, {"replica": partner}):
        pl.semaphore_signal(barrier, inc=1, device_id=peer, device_id_type=MESH_ID)
    pl.semaphore_wait(barrier, 3)

    def window(array, owner, chunk):
        rows = owned[array].shape[0]
        _, row, height, column, columns = chunk
        return full[array].at[pl.ds(owner * rows + row, height), pl.ds(column, columns)]

    def own(array, chunk):
        _, row, height, column, columns = chunk
        return owned[array].at[pl.ds(row, height), pl.ds(column, columns)]

    def remote(source, target, out_sem, in_sem, device):
        return pltpu.make_async_remote_copy(
            src_ref=source,
            dst_ref=target,
            send_sem=out_sem,
            recv_sem=in_sem,
            device_id=device,
            device_id_type=MESH_ID,
        )

    chunks = [(half, chunk) for half in range(2) for chunk in halves[half]]

    def near(k):
        chunk = chunks[k][1]
        array = chunk[0]
        return remote(
            own(array, chunk),
            window(array, shard, chunk),
            near_out.at[k],
            near_in.at[k],
            {"shard": sibling},
        )

    def far(k):
        chunk = chunks[k][1]
        array = chunk[0]
        return remote(
            own(array, chunk),
            window(array, shard, chunk),
            far_out.at[k],
            far_in.at[k],
            {"shard": across},
        )

    def sideways(k):
        chunk = chunks[k][1]
        part = window(chunk[0], across, chunk)
        return remote(part, part, side_out.at[k], far_in.at[k], {"replica": partner})

    def onward(k):
        chunk = chunks[k][1]
        part = window(chunk[0], across, chunk)
        return remote(part, part, pass_out.at[k], pass_in.at[k], {"shard": sibling})

    def keep(array):
        rows = owned[array].shape[0]
        return pltpu.make_async_copy(
            owned[array], full[array].at[pl.ds(shard * rows, rows), :], local.at[array]
        )

    indices = [[k for k, entry in enumerate(chunks) if entry[0] == half] for half in range(2)]

    def flow(half):
        mine, others = indices[half], indices[1 - half]
        for k in mine:
            far(k).start()
        for k in mine + others:
            near(k).start()
        for array in range(4):
            keep(array).start()
        for j in range(max(len(mine), len(others) + 1)):
            if j < len(mine):
                far(mine[j]).wait_recv()
                sideways(mine[j]).start()
                onward(mine[j]).start()
            if 0 <= j - 1 < len(others):
                far(others[j - 1]).wait_recv()
                onward(others[j - 1]).start()
        for k in mine:
            far(k).wait_send()
            sideways(k).wait_send()
        for k in mine + others:
            near(k).wait()
            onward(k).wait()
        for array in range(4):
            keep(array).wait()

    for half in range(2):
        pl.when(parity == half)(functools.partial(flow, half))


def gather_weights(owned):
    owners = lax.axis_size("shard")
    cuts = split_pieces([weight.shape for weight in owned])
    halves = [[cut for cut in cuts if cut[0] != 2], [cut for cut in cuts if cut[0] == 2]]
    count = len(cuts)
    anywhere = pl.BlockSpec(memory_space=pl.ANY)
    return pl.pallas_call(
        functools.partial(gather_kernel, halves),
        out_shape=[
            jax.ShapeDtypeStruct((owners * weight.shape[0], weight.shape[1]), weight.dtype)
            for weight in owned
        ],
        in_specs=[anywhere] * 4,
        out_specs=[anywhere] * 4,
        scratch_shapes=[pltpu.SemaphoreType.DMA((count,))] * 7 + [pltpu.SemaphoreType.DMA((4,))],
        compiler_params=pltpu.CompilerParams(collective_id=2, has_side_effects=True),
        cost_estimate=pl.CostEstimate(flops=0, bytes_accessed=2**24, transcendentals=0),
    )(*owned)


def from_behind(block, axis, distance):
    devices = range(lax.axis_size(axis))
    route = [(i - distance, i) for i in devices if i - distance in devices]
    return lax.ppermute(block, axis, route)


def shards(
    inputs,
    segments,
    cotangent,
    attn_gain,
    qkv_weight,
    out_weight,
    ffn_gain,
    gate_up_weight,
    down_weight,
):
    sections = lax.axis_size("section")
    section_index = lax.axis_index("section")
    qkv_full, out_full, gate_up_full, down_full = gather_weights(
        (qkv_weight[0], out_weight[0], gate_up_weight[0], down_weight[0])
    )
    weights = (attn_gain[0], qkv_full, out_full, ffn_gain[0], gate_up_full, down_full)
    geom = geometry(segments)
    layer_in = inputs
    for tick in range(sections):
        if tick > 0:
            arrived = from_behind(outgoing, "section", 1)
            layer_in = jnp.where(section_index == 0, inputs, arrived)
        result, stored = layer_forward(layer_in, weights, geom)
        outgoing = result.astype(jnp.bfloat16)
    incoming = cotangent
    for tick in range(sections):
        if tick > 0:
            arrived = from_behind(passed, "section", -1)
            incoming = jnp.where(section_index == sections - 1, cotangent, arrived)
        grad_stream, gain_terms, operands = layer_backward(
            incoming.astype(jnp.float32), weights, geom, stored
        )
        passed = grad_stream.astype(jnp.bfloat16)
    sums, gain_sums = reduce_gradients(operands, gain_terms, lax.axis_size("replica"))
    down_sum, gate_up_sum, out_sum, qkv_sum = sums
    return (
        outgoing[None],
        passed[None],
        gain_sums[0],
        qkv_sum[None],
        out_sum[None],
        gain_sums[1],
        gate_up_sum[None],
        down_sum[None],
    )


def solution(mesh):
    return jax.shard_map(
        shards,
        mesh=mesh,
        in_specs=(
            P(("shard", "replica"), None),
            P(("shard", "replica"), None),
            P(("shard", "replica"), None),
            P("section", None),
            P("section", "shard", None),
            P("section", "shard", None),
            P("section", None),
            P("section", "shard", None),
            P("section", "shard", None),
        ),
        out_specs=(
            P("section", ("shard", "replica"), None),
            P("section", ("shard", "replica"), None),
            P("section", "shard"),
            P("section", "shard", None),
            P("section", "shard", None),
            P("section", "shard"),
            P("section", "shard", None),
            P("section", "shard", None),
        ),
        check_vma=False,
    )
```

```python
import functools
import math

import jax
import jax.numpy as jnp
from jax import lax
from jax.experimental import pallas as pl
from jax.experimental.pallas import tpu as pltpu
from jax.sharding import PartitionSpec as P

HEADS = 9
KV = 3
HD = 64
FF = 1536


norm_epsilon = 1e-05
rope_base = 100000.0
masked_value = -1e30


def geometry(segment_ids):
    count_cols = segment_ids.shape[-1]
    column = jnp.arange(count_cols, dtype=jnp.int32)
    previous = jnp.concatenate([segment_ids[..., :1], segment_ids[..., :-1]], axis=-1)
    doc_marks = jnp.where(segment_ids != previous, column, 0)
    doc_starts = lax.cummax(doc_marks, axis=doc_marks.ndim - 1)
    positions = (column - doc_starts).astype(jnp.float32)
    allowed = (segment_ids[..., :, None] == segment_ids[..., None, :]) & (
        column[:, None] >= column[None, :]
    )
    half_width = HD // 2
    frequency = jnp.exp(
        -(jnp.arange(half_width, dtype=jnp.float32) * (2.0 / HD)) * math.log(rope_base)
    )
    angles = positions[..., None] * frequency
    cosine_half = jnp.cos(angles).reshape(-1, half_width)
    sine_half = jnp.sin(angles).reshape(-1, half_width)
    cosine_table = jnp.concatenate([cosine_half] * 4, axis=-1)
    sine_table = jnp.concatenate([-sine_half, sine_half] * 2, axis=-1)
    return (allowed.astype(jnp.int32), cosine_table, sine_table)


GROUP = HEADS // KV
ROTATED = (HEADS + KV) * HD


def halves_swapped(block):
    lane = lax.broadcasted_iota(jnp.int32, block.shape, 1)
    ahead = pltpu.roll(block, 128 - HD // 2, 1)
    behind = pltpu.roll(block, HD // 2, 1)
    return jnp.where(lane % HD < HD // 2, ahead, behind)


def head_rows(ref, start, length, kv_head):
    return jnp.concatenate(
        [
            ref[start : start + length, head * HD : (head + 1) * HD]
            for head in range(kv_head * GROUP, (kv_head + 1) * GROUP)
        ],
        axis=0,
    )


def matmul(left, right, left_dim, right_dim):
    return lax.dot_general(
        left, right, (((left_dim,), (right_dim,)), ((), ())), preferred_element_type=jnp.float32
    )


def attention_kernel(projected_ref, cosine_ref, sine_ref, allowed_ref, heads_ref, probs_ref, out_ref):
    groups, length = allowed_ref.shape[:2]
    for column in range(0, ROTATED, 128):
        block = projected_ref[:, column : column + 128]
        turned = block * cosine_ref[...] + halves_swapped(block) * sine_ref[...]
        heads_ref[:, column : column + 128] = turned.astype(jnp.bfloat16)
    heads_ref[:, ROTATED:] = projected_ref[:, ROTATED:].astype(jnp.bfloat16)
    for group in range(groups):
        start = group * length
        allowed = jnp.concatenate([allowed_ref[group]] * GROUP, axis=0) > 0
        for k in range(KV):
            queries = head_rows(heads_ref, start, length, k)
            keys = heads_ref[start : start + length, (HEADS + k) * HD : (HEADS + k + 1) * HD]
            values = heads_ref[
                start : start + length, ROTATED + k * HD : ROTATED + (k + 1) * HD
            ]
            scores = matmul(queries, keys, 1, 1) * HD ** (-0.5)
            scores = jnp.where(allowed, scores, masked_value)
            row_exp = jnp.exp(scores - jnp.max(scores, axis=-1, keepdims=True))
            probs = row_exp / jnp.sum(row_exp, axis=-1, keepdims=True)
            probs_ref[group, k] = probs
            attended = matmul(probs.astype(jnp.bfloat16), values, 1, 0).astype(jnp.bfloat16)
            for r in range(GROUP):
                head = k * GROUP + r
                out_ref[start : start + length, head * HD : (head + 1) * HD] = attended[
                    r * length : (r + 1) * length
                ]


def attention_back_kernel(
    heads_ref, probs_ref, grad_ref, cosine_ref, sine_ref, out_ref, turned_ref
):
    groups = probs_ref.shape[0]
    length = probs_ref.shape[3]
    for group in range(groups):
        start = group * length
        rows = slice(start, start + length)
        for k in range(KV):
            queries = head_rows(heads_ref, start, length, k)
            grad_att = head_rows(grad_ref, start, length, k).astype(jnp.bfloat16)
            keys = heads_ref[rows, (HEADS + k) * HD : (HEADS + k + 1) * HD]
            values = heads_ref[rows, ROTATED + k * HD : ROTATED + (k + 1) * HD]
            probs = probs_ref[group, k]
            grad_values = matmul(probs.astype(jnp.bfloat16), grad_att, 0, 0)
            grad_probs = matmul(grad_att, values, 1, 1)
            inner = jnp.sum(probs * grad_probs, axis=-1, keepdims=True)
            grad_scores = (probs * (grad_probs - inner)).astype(jnp.bfloat16)
            grad_query = matmul(grad_scores, keys, 1, 0) * HD ** (-0.5)
            grad_keys = matmul(grad_scores, queries, 0, 0) * HD ** (-0.5)
            for r in range(GROUP):
                head = k * GROUP + r
                turned_ref[rows, head * HD : (head + 1) * HD] = grad_query[
                    r * length : (r + 1) * length
                ]
            turned_ref[rows, (HEADS + k) * HD : (HEADS + k + 1) * HD] = grad_keys
            out_ref[rows, ROTATED + k * HD : ROTATED + (k + 1) * HD] = grad_values.astype(
                jnp.bfloat16
            )
    for column in range(0, ROTATED, 128):
        block = turned_ref[:, column : column + 128]
        back = block * cosine_ref[...] - halves_swapped(block) * sine_ref[...]
        out_ref[:, column : column + 128] = back.astype(jnp.bfloat16)


def local_call(kernel, operands, outputs, scratch=()):
    vmem = pl.BlockSpec(memory_space=pltpu.VMEM)
    return pl.pallas_call(
        kernel,
        out_shape=[jax.ShapeDtypeStruct(shape, kind) for shape, kind in outputs],
        in_specs=[vmem] * len(operands),
        out_specs=[vmem] * len(outputs),
        scratch_shapes=list(scratch),
        compiler_params=pltpu.CompilerParams(vmem_limit_bytes=32 * 2**20),
    )(*operands)


def attention(projected, geom):
    allowed, cosine_table, sine_table = geom
    groups, length = allowed.shape[:2]
    tokens = projected.shape[0]
    return local_call(
        attention_kernel,
        (projected, cosine_table, sine_table, allowed),
        (
            (projected.shape, jnp.bfloat16),
            ((groups, KV, GROUP * length, length), jnp.float32),
            ((tokens, HEADS * HD), jnp.bfloat16),
        ),
    )


def attention_back(heads, probs, grad_att, geom):
    allowed, cosine_table, sine_table = geom
    return local_call(
        attention_back_kernel,
        (heads, probs, grad_att, cosine_table, sine_table),
        ((heads.shape, jnp.bfloat16),),
        [pltpu.VMEM((heads.shape[0], ROTATED), jnp.float32)],
    )[0]


def norm_back(residual, stream, inverse, gain_row, grad_out):
    grad_gain = jnp.sum(grad_out * stream * inverse, axis=0)
    grad_hat = grad_out * gain_row
    inner = jnp.mean(grad_hat * stream, axis=-1, keepdims=True)
    return (residual + inverse * (grad_hat - stream * inverse * inverse * inner), grad_gain)


def layer_forward(layer_in, weights, geom):
    gain_attn, qkv_layer, out_layer, gain_ffn, gate_up_layer, down_layer = weights
    stream = layer_in.astype(jnp.float32)
    inv_attn = lax.rsqrt(jnp.mean(stream * stream, axis=-1, keepdims=True) + norm_epsilon)
    normed = (stream * inv_attn * gain_attn).astype(jnp.bfloat16)
    projected = jnp.dot(normed, qkv_layer, preferred_element_type=jnp.float32)
    heads, attn_probs, attended = attention(projected, geom)
    middle = stream + jnp.dot(attended, out_layer, preferred_element_type=jnp.float32)
    inv_ffn = lax.rsqrt(jnp.mean(middle * middle, axis=-1, keepdims=True) + norm_epsilon)
    ffn_normed = (middle * inv_ffn * gain_ffn).astype(jnp.bfloat16)
    gate_up = jnp.dot(ffn_normed, gate_up_layer, preferred_element_type=jnp.float32)
    hidden = (jax.nn.silu(gate_up[:, :FF]) * gate_up[:, FF:]).astype(jnp.bfloat16)
    result = middle + jnp.dot(hidden, down_layer, preferred_element_type=jnp.float32)
    stored = (
        stream,
        inv_attn,
        normed,
        heads,
        attn_probs,
        attended,
        middle,
        inv_ffn,
        ffn_normed,
        gate_up,
        hidden,
    )
    return (result, stored)


def layer_backward(incoming, weights, geom, stored):
    gain_attn, qkv_layer, out_layer, gain_ffn, gate_up_layer, down_layer = weights
    (
        stream,
        inv_attn,
        normed,
        heads,
        attn_probs,
        attended,
        middle,
        inv_ffn,
        ffn_normed,
        gate_up,
        hidden,
    ) = stored
    out_rounded = incoming.astype(jnp.bfloat16)
    grad_hidden = jnp.einsum(
        "sd,fd->sf", out_rounded, down_layer, preferred_element_type=jnp.float32
    )
    gate_part = gate_up[:, :FF]
    up_part = gate_up[:, FF:]
    gate_sigmoid = jax.nn.sigmoid(gate_part)
    gate_silu = gate_part * gate_sigmoid
    grad_gate = grad_hidden * up_part * gate_sigmoid * (1.0 + gate_part * (1.0 - gate_sigmoid))
    grad_gu = jnp.concatenate([grad_gate, grad_hidden * gate_silu], axis=-1).astype(jnp.bfloat16)
    grad_fnorm = jnp.einsum("se,de->sd", grad_gu, gate_up_layer, preferred_element_type=jnp.float32)
    grad_middle, grad_gain_ffn = norm_back(incoming, middle, inv_ffn, gain_ffn, grad_fnorm)
    mid_rounded = grad_middle.astype(jnp.bfloat16)
    grad_att = jnp.einsum("sd,cd->sc", mid_rounded, out_layer, preferred_element_type=jnp.float32)
    grad_projected = attention_back(heads, attn_probs, grad_att, geom)
    grad_normed = jnp.einsum(
        "se,de->sd", grad_projected, qkv_layer, preferred_element_type=jnp.float32
    )
    grad_stream, grad_gain_attn = norm_back(grad_middle, stream, inv_attn, gain_attn, grad_normed)
    operands = (
        (hidden, out_rounded),
        (ffn_normed, grad_gu),
        (attended, mid_rounded),
        (normed, grad_projected),
    )
    return (grad_stream, (grad_gain_attn, grad_gain_ffn), operands)


GAIN_ROWS = 16
MESH_ID = pl.DeviceIdType.MESH


def split_pieces(shapes):
    pieces = []
    for array, (rows, columns) in enumerate(shapes):
        row_step = 128 if rows > 144 and rows % 128 == 0 else rows
        column_step = 512 if columns > 1024 else columns
        for row in range(0, rows, row_step):
            for column in range(0, columns, column_step):
                pieces.append((array, row, row_step, column, column_step))
    return pieces


def reduce_kernel(pieces, replicas, *refs):
    count = len(pieces) + 1
    lefts, rights, gain_ref = refs[0:4], refs[4:8], refs[8]
    outs, gain_out = refs[9:13], refs[13]
    scratch = refs[14:]
    groups = [scratch[k * count : (k + 1) * count] for k in range(8)]
    send_a, recv_a, keep_a, send_b, recv_b, send_c, recv_c, recv_x = groups
    totals = scratch[8 * count : 9 * count]
    sems = scratch[9 * count :]
    a_out, a_in, b_out, b_in, c_out, c_in, x_out, x_in = sems

    shard = lax.axis_index("shard")
    place = lax.axis_index("replica")
    core = shard % 2
    row_y = shard // 2
    sibling = row_y * 2 + (1 - core)
    across = (1 - row_y) * 2 + core
    half = replicas // 2
    is_left = place < half
    inward = jnp.where(is_left, place + 1, place - 1)
    outward = jnp.where(is_left, place - 1, place + 1)
    is_middle = (place == half - 1) | (place == half)
    has_outer = (place > 0) & (place < replicas - 1)

    barrier = pltpu.get_barrier_semaphore()
    for peer in (sibling, across):
        pl.semaphore_signal(barrier, inc=1, device_id={"shard": peer}, device_id_type=MESH_ID)
    pl.semaphore_signal(barrier, inc=1, device_id={"replica": inward}, device_id_type=MESH_ID)

    @pl.when(has_outer)
    def _():
        pl.semaphore_signal(barrier, inc=1, device_id={"replica": outward}, device_id_type=MESH_ID)

    pl.semaphore_wait(barrier, jnp.where(has_outer, 4, 3))

    def copy(source, target, out_sem, in_sem, device):
        return pltpu.make_async_remote_copy(
            src_ref=source,
            dst_ref=target,
            send_sem=out_sem,
            recv_sem=in_sem,
            device_id=device,
            device_id_type=MESH_ID,
        )

    def copy_a(p):
        return copy(send_a[p], recv_a[p], a_out.at[p], a_in.at[p], {"shard": sibling})

    def copy_b(p):
        return copy(send_b[p], recv_b[p], b_out.at[p], b_in.at[p], {"shard": across})

    def copy_c(p):
        return copy(send_c[p], recv_c[p], c_out.at[p], c_in.at[p], {"replica": inward})

    def copy_middle(p):
        return copy(send_c[p], recv_x[p], c_out.at[p], x_in.at[p], {"replica": inward})

    def copy_x(p):
        return copy(totals[p], recv_x[p], x_out.at[p], x_in.at[p], {"replica": outward})

    def term(p, owner):
        if p == count - 1:
            return gain_ref[owner]
        array, row, rows, column, columns = pieces[p]
        return jnp.dot(
            lefts[array][owner, row : row + rows, :],
            rights[array][:, column : column + columns],
            preferred_element_type=jnp.float32,
        )

    def stage_a(p):
        for y in range(2):
            send_a[p][y] = term(p, 2 * y + (1 - core)).astype(jnp.bfloat16)
        copy_a(p).start()
        for y in range(2):
            keep_a[p][y] = term(p, 2 * y + core)

    def stage_b(p):
        copy_a(p).wait_recv()
        other = 1 - row_y
        send_b[p][...] = (keep_a[p][other] + recv_a[p][other].astype(jnp.float32)).astype(
            jnp.bfloat16
        )
        copy_b(p).start()

    def stage_c(p):
        copy_b(p).wait_recv()
        keep_a[p][0] = (
            keep_a[p][row_y]
            + recv_a[p][row_y].astype(jnp.float32)
            + recv_b[p][...].astype(jnp.float32)
        )

        @pl.when(has_outer)
        def _():
            copy_c(p).wait_recv()
            keep_a[p][0] = keep_a[p][0] + recv_c[p][...].astype(jnp.float32)

        send_c[p][...] = keep_a[p][0].astype(jnp.bfloat16)

        @pl.when(is_middle)
        def _():
            copy_middle(p).start()

        @pl.when(jnp.logical_not(is_middle))
        def _():
            copy_c(p).start()

    def finish(p):
        @pl.when(has_outer)
        def _():
            copy_x(p).start()

        total = totals[p][...].astype(jnp.float32)
        if p == count - 1:
            gain_out[...] = total
        else:
            array, row, rows, column, columns = pieces[p]
            outs[array][row : row + rows, column : column + columns] = total

    def stage_middle(p):
        copy_x(p).wait_recv()
        totals[p][...] = (
            send_c[p][...].astype(jnp.float32) + recv_x[p][...].astype(jnp.float32)
        ).astype(jnp.bfloat16)
        finish(p)

    def stage_outer(p):
        copy_x(p).wait_recv()
        totals[p][...] = recv_x[p][...]
        finish(p)

    lag_b, lag_c, lag_d, lag_outer = 2, 5, 8, 12
    for step in range(count + lag_outer):
        if step < count:
            stage_a(step)
        if 0 <= step - lag_b < count:
            stage_b(step - lag_b)
        if 0 <= step - lag_c < count:
            stage_c(step - lag_c)
        if 0 <= step - lag_d < count:
            pl.when(is_middle)(functools.partial(stage_middle, step - lag_d))
        if 0 <= step - lag_outer < count:
            pl.when(jnp.logical_not(is_middle))(functools.partial(stage_outer, step - lag_outer))
    for p in range(count):
        copy_a(p).wait_send()
        copy_b(p).wait_send()
        copy_c(p).wait_send()

        @pl.when(has_outer)
        def _(p=p):
            copy_x(p).wait_send()


def reduce_gradients(operands, gains, replicas):
    owners = lax.axis_size("shard")
    lefts, rights, shapes = [], [], []
    for left, right in operands:
        tokens, rows = left.shape
        lefts.append(left.T.reshape(owners, rows // owners, tokens))
        rights.append(right)
        shapes.append((rows // owners, right.shape[1]))
    width = gains[0].shape[0] // owners
    packed = jnp.stack([gain.reshape(owners, width) for gain in gains], axis=1)
    packed = jnp.pad(packed, ((0, 0), (0, GAIN_ROWS - 2), (0, 256 - width)))
    pieces = split_pieces(shapes)
    extents = [(rows, columns) for _, _, rows, _, columns in pieces] + [(GAIN_ROWS, 256)]
    low, full = jnp.bfloat16, jnp.float32
    scratch = []
    for lead, kind in (
        ((2,), low),
        ((2,), low),
        ((2,), full),
        ((), low),
        ((), low),
        ((), low),
        ((), low),
        ((), low),
        ((), low),
    ):
        scratch += [pltpu.VMEM(lead + extent, kind) for extent in extents]
    scratch += [pltpu.SemaphoreType.DMA((len(extents),))] * 8
    vmem = pl.BlockSpec(memory_space=pltpu.VMEM)
    flops = sum(2 * left.shape[0] * left.shape[1] * right.shape[1] for left, right in operands)
    results = pl.pallas_call(
        functools.partial(reduce_kernel, pieces, replicas),
        out_shape=[jax.ShapeDtypeStruct(shape, full) for shape in shapes]
        + [jax.ShapeDtypeStruct((GAIN_ROWS, 256), full)],
        in_specs=[vmem] * 9,
        out_specs=[vmem] * 5,
        scratch_shapes=scratch,
        compiler_params=pltpu.CompilerParams(
            collective_id=1, has_side_effects=True, vmem_limit_bytes=58 * 2**20
        ),
        cost_estimate=pl.CostEstimate(flops=flops, bytes_accessed=2 * 2**20, transcendentals=0),
    )(*lefts, *rights, packed)
    gain_rows = results[4]
    return results[:4], [gain_rows[i : i + 1, :width] for i in range(2)]


def gather_kernel(halves, *refs):
    owned, full = refs[0:4], refs[4:8]
    near_out, near_in, far_out, far_in, cross_out, cross_in, side_out, edge_out, local = refs[8:]
    shard = lax.axis_index("shard")
    place = lax.axis_index("replica")
    core = shard % 2
    row_y = shard // 2
    sibling = row_y * 2 + (1 - core)
    across = (1 - row_y) * 2 + core
    diagonal = (1 - row_y) * 2 + (1 - core)
    parity = place % 2
    partner = place + 1 - 2 * parity

    barrier = pltpu.get_barrier_semaphore()
    for peer in (
        {"shard": sibling},
        {"shard": across},
        {"shard": diagonal},
        {"replica": partner},
    ):
        pl.semaphore_signal(barrier, inc=1, device_id=peer, device_id_type=MESH_ID)
    pl.semaphore_wait(barrier, 4)

    def window(array, owner, chunk):
        rows = owned[array].shape[0]
        _, row, height, column, columns = chunk
        return full[array].at[pl.ds(owner * rows + row, height), pl.ds(column, columns)]

    def own(array, chunk):
        _, row, height, column, columns = chunk
        return owned[array].at[pl.ds(row, height), pl.ds(column, columns)]

    def remote(source, target, out_sem, in_sem, device):
        return pltpu.make_async_remote_copy(
            src_ref=source,
            dst_ref=target,
            send_sem=out_sem,
            recv_sem=in_sem,
            device_id=device,
            device_id_type=MESH_ID,
        )

    chunks = [(half, chunk) for half in range(2) for chunk in halves[half]]

    def near(k):
        chunk = chunks[k][1]
        array = chunk[0]
        return remote(
            own(array, chunk),
            window(array, shard, chunk),
            near_out.at[k],
            near_in.at[k],
            {"shard": sibling},
        )

    def far(k):
        chunk = chunks[k][1]
        array = chunk[0]
        return remote(
            own(array, chunk),
            window(array, shard, chunk),
            far_out.at[k],
            far_in.at[k],
            {"shard": across},
        )

    def sideways(k):
        chunk = chunks[k][1]
        part = window(chunk[0], across, chunk)
        return remote(part, part, side_out.at[k], far_in.at[k], {"replica": partner})

    def cross(k):
        chunk = chunks[k][1]
        array = chunk[0]
        return remote(
            own(array, chunk),
            window(array, shard, chunk),
            cross_out.at[k],
            cross_in.at[k],
            {"shard": diagonal},
        )

    def edge(k):
        chunk = chunks[k][1]
        part = window(chunk[0], diagonal, chunk)
        return remote(part, part, edge_out.at[k], cross_in.at[k], {"replica": partner})

    def keep(array):
        rows = owned[array].shape[0]
        return pltpu.make_async_copy(
            owned[array], full[array].at[pl.ds(shard * rows, rows), :], local.at[array]
        )

    indices = [[k for k, entry in enumerate(chunks) if entry[0] == half] for half in range(2)]

    def flow(half):
        mine, others = indices[half], indices[1 - half]
        for k in mine:
            far(k).start()
            cross(k).start()
        for k in mine + others:
            near(k).start()
        for array in range(4):
            keep(array).start()
        for k in mine:
            far(k).wait_recv()
            sideways(k).start()
            cross(k).wait_recv()
            edge(k).start()
        for k in others:
            far(k).wait_recv()
            cross(k).wait_recv()
        for k in mine:
            far(k).wait_send()
            cross(k).wait_send()
            sideways(k).wait_send()
            edge(k).wait_send()
        for k in mine + others:
            near(k).wait()
        for array in range(4):
            keep(array).wait()

    for half in range(2):
        pl.when(parity == half)(functools.partial(flow, half))


def gather_weights(owned):
    owners = lax.axis_size("shard")
    cuts = split_pieces([weight.shape for weight in owned])
    halves = [[cut for cut in cuts if cut[0] != 2], [cut for cut in cuts if cut[0] == 2]]
    count = len(cuts)
    anywhere = pl.BlockSpec(memory_space=pl.ANY)
    return pl.pallas_call(
        functools.partial(gather_kernel, halves),
        out_shape=[
            jax.ShapeDtypeStruct((owners * weight.shape[0], weight.shape[1]), weight.dtype)
            for weight in owned
        ],
        in_specs=[anywhere] * 4,
        out_specs=[anywhere] * 4,
        scratch_shapes=[pltpu.SemaphoreType.DMA((count,))] * 8 + [pltpu.SemaphoreType.DMA((4,))],
        compiler_params=pltpu.CompilerParams(collective_id=2, has_side_effects=True),
        cost_estimate=pl.CostEstimate(flops=0, bytes_accessed=2**24, transcendentals=0),
    )(*owned)


def from_behind(block, axis, distance):
    devices = range(lax.axis_size(axis))
    route = [(i - distance, i) for i in devices if i - distance in devices]
    return lax.ppermute(block, axis, route)


def shards(
    inputs,
    segments,
    cotangent,
    attn_gain,
    qkv_weight,
    out_weight,
    ffn_gain,
    gate_up_weight,
    down_weight,
):
    sections = lax.axis_size("section")
    section_index = lax.axis_index("section")
    qkv_full, out_full, gate_up_full, down_full = gather_weights(
        (qkv_weight[0], out_weight[0], gate_up_weight[0], down_weight[0])
    )
    weights = (attn_gain[0], qkv_full, out_full, ffn_gain[0], gate_up_full, down_full)
    geom = geometry(segments)
    layer_in = inputs
    for tick in range(sections):
        if tick > 0:
            arrived = from_behind(outgoing, "section", 1)
            layer_in = jnp.where(section_index == 0, inputs, arrived)
        result, stored = layer_forward(layer_in, weights, geom)
        outgoing = result.astype(jnp.bfloat16)
    incoming = cotangent
    for tick in range(sections):
        if tick > 0:
            arrived = from_behind(passed, "section", -1)
            incoming = jnp.where(section_index == sections - 1, cotangent, arrived)
        grad_stream, gain_terms, operands = layer_backward(
            incoming.astype(jnp.float32), weights, geom, stored
        )
        passed = grad_stream.astype(jnp.bfloat16)
    sums, gain_sums = reduce_gradients(operands, gain_terms, lax.axis_size("replica"))
    down_sum, gate_up_sum, out_sum, qkv_sum = sums
    return (
        outgoing[None],
        passed[None],
        gain_sums[0],
        qkv_sum[None],
        out_sum[None],
        gain_sums[1],
        gate_up_sum[None],
        down_sum[None],
    )


def solution(mesh):
    return jax.shard_map(
        shards,
        mesh=mesh,
        in_specs=(
            P(("shard", "replica"), None),
            P(("shard", "replica"), None),
            P(("shard", "replica"), None),
            P("section", None),
            P("section", "shard", None),
            P("section", "shard", None),
            P("section", None),
            P("section", "shard", None),
            P("section", "shard", None),
        ),
        out_specs=(
            P("section", ("shard", "replica"), None),
            P("section", ("shard", "replica"), None),
            P("section", "shard"),
            P("section", "shard", None),
            P("section", "shard", None),
            P("section", "shard"),
            P("section", "shard", None),
            P("section", "shard", None),
        ),
        check_vma=False,
    )
```
